32 devices in a mesh: chain: 2 (over core), sector: 16 (over z, y, x).
Axes of the slice: x: 2, y: 2, z: 4, core: 2. Of those that a mesh axis runs over, the one named last changes fastest.
Arguments:
- env_first: bfloat16 [2, 16, 15, 128, 128], P(None, 'sector'), may hold values from -6 to 6
- states: bfloat16 [2, 2, 4, 16, 128, 128], P('chain', None, None, 'sector'), may hold values from -0.5 to 0.5
- mpo: bfloat16 [2, 4, 15, 15], P('chain'), may hold values from -1.5 to 1.5
- block_rows: int32 [2, 16], P('chain', 'sector'), may hold values from 1 to 128, 1024 in all within a row
- present: int32 [2, 4, 16], P('chain', None, 'sector'), may hold values 0 or 1
Outputs:
- env_out: bfloat16 [2, 2, 16, 15, 128, 128], P('chain', None, 'sector')
The draws below stay inside these ranges and needn't reach their ends.
Inputs may be any that keep to these rules, and one draw needn't show every extreme that they name: `block_rows`: in each site's row the 16 live sizes add up to 1024, and one of them equals 128.
All inputs are finite; a program needn't handle non-finite values. No bound on the sum of `block_rows` or of `present` on one device may be relied on, other than what follows from the above.
Results may differ from the reference program's by a relative error of at most 0.008.
Values may be sent and summed in bfloat16 or wider, within the bound.
No kernel may reach another device: no remote copies, remote signals or barrier semaphores. Data moves between devices by JAX's collectives and lax.ppermute only.
A program may use at most 128 MiB of HBM per device.

```python
import math
import jax
import jax.numpy as jnp
import numpy as np
from jax import lax

BLK = 128
W = 15
D_PHYS = 4
TARGETS = 2
QD = 4
SECTORS = 16
SITES = 2


def place_ends(array, key, smallest, largest):
    place = [jax.random.randint(jax.random.fold_in(key, axis), (), 0, length) for axis, length in enumerate(array.shape)]
    widest = array.shape.index(max(array.shape))
    next_to = place[:widest] + [(place[widest] + 1) % array.shape[widest]] + place[widest + 1:]
    return array.at[tuple(place)].set(smallest).at[tuple(next_to)].set(largest)


def shard_levels(own_key, shape, shards, smallest, top_value):
    level, own = 1.0, jax.random.fold_in(own_key, 6)
    for position, parts in shards:
        steps = jnp.exp(jax.random.uniform(jax.random.fold_in(own, position), (parts,), jnp.float32, smallest / len(shards), top_value / len(shards)))
        level = level * jnp.repeat(steps, shape[position] // parts).reshape([-1 if axis == position else 1 for axis in range(len(shape))])
    return level


def split_up(amount, total, limit, lean):
    weights = [(1 << 20) // math.isqrt(grade ** lean) + 1 for grade in range(2, amount + 1)]
    rest, holding = total - limit - (amount - 1), [1] * (amount - 1)
    while rest > 0:
        free = [i for i in range(amount - 1) if holding[i] < limit]
        pool, left = sum([weights[i] for i in free]), rest
        for i in free:
            more = min(limit - holding[i], max(1, left * weights[i] // pool), rest)
            holding[i] = holding[i] + more
            rest = rest - more
    return np.array([limit] + holding)


def uneven_parts(key, number_of, total, most, lean):
    if number_of == 2:
        one = jax.random.randint(key, (), max(1, total - most), min(most, total - 1) + 1)
        return jnp.stack([one, total - one])
    lengths = jnp.asarray(split_up(number_of, total, most, lean), jnp.int32)
    pairs = (number_of - 1) // 2
    donor, sink = lengths[1:1 + 2 * pairs:2], lengths[2:2 + 2 * pairs:2]
    margin = jnp.minimum(donor - 1, most - sink)
    passed = jax.random.randint(jax.random.fold_in(key, 1), (pairs,), 0, 1 << 20) % (margin + 1)
    lengths = lengths.at[1:1 + 2 * pairs:2].set(donor - passed).at[2:2 + 2 * pairs:2].set(sink + passed)
    return lengths[jax.random.permutation(jax.random.fold_in(key, 2), number_of)]


def centred(rng, dims, deviation, bound, split=(), kind=jnp.bfloat16):
    gain = shard_levels(rng, dims, split, -0.22, 0.18) if split else 1.0
    entries = jax.random.normal(rng, dims, jnp.float32) * deviation * gain
    return jnp.minimum(jnp.maximum(entries, -bound), bound).astype(kind)


def setup_inputs(seed: int = 0) -> dict:
    streams_of = jax.random.split(jax.random.key(seed), 6)
    return {
        "env_first": centred(streams_of[0], (TARGETS, SECTORS, W, BLK, BLK), 1.0, 6.0, ((1, 16),)),
        "states": centred(streams_of[1], (SITES, TARGETS, D_PHYS, SECTORS, BLK, BLK), BLK ** -0.5, 0.5, ((0, 2), (3, 16))),
        "mpo": centred(streams_of[2], (SITES, D_PHYS, W, W), W ** -0.5, 1.5, ((0, 2),)),
        "block_rows": jax.vmap(lambda own: uneven_parts(own, SECTORS, SECTORS * BLK // 2, BLK, 2))(jax.random.split(streams_of[3], SITES)).reshape((SITES, SECTORS)).astype(jnp.int32),
        "present": place_ends((jax.random.randint(streams_of[4], (SITES, D_PHYS, SECTORS), 0, 4) < 3).astype(jnp.int32), jax.random.fold_in(streams_of[4], 1), 0, 1),
    }


def shift_sectors(values, offset):
    sector_count = values.shape[1]
    return jnp.concatenate([jnp.zeros_like(values[:, :offset]), values[:, :sector_count - offset]], axis=1)


def reference(env_first, states, mpo, block_rows, present):
    environment = env_first
    sector_ids = jnp.arange(SECTORS)
    inside_grid = (sector_ids % QD < QD - 1).astype(jnp.float32)
    state_ids = jnp.arange(D_PHYS)
    collected = []
    for site_index in range(SITES):
        blocks = states[site_index].astype(jnp.float32)
        projected = jnp.einsum("tkwab,tskbc->tskwac", environment.astype(jnp.float32), blocks).astype(jnp.bfloat16)
        projected = lax.optimization_barrier(projected).astype(jnp.float32)
        sandwich = jnp.einsum("tskad,tskwac->tskwdc", blocks, projected)
        coupled = jnp.einsum("tskwdc,swv->tskvdc", sandwich, mpo[site_index].astype(jnp.float32), precision=lax.Precision.HIGHEST)
        keep_mask = present[site_index].astype(jnp.float32) * jnp.where(state_ids[:, None] >= 2, inside_grid[None, :], 1.0)
        partials = (coupled * keep_mask[None, :, :, None, None, None]).astype(jnp.bfloat16)
        partials = lax.optimization_barrier(partials).astype(jnp.float32)
        summed = partials[:, 0] + shift_sectors(partials[:, 2], 1) + shift_sectors(partials[:, 1], QD) + shift_sectors(partials[:, 3], QD + 1)
        live_rows = jnp.arange(BLK)[None, :] < block_rows[site_index][:, None]
        live_mask = live_rows[:, None, :, None] & live_rows[:, None, None, :]
        environment = jnp.where(live_mask[None], summed, 0.0).astype(jnp.bfloat16)
        collected.append(environment)
    return jnp.stack(collected)
```

```python
import functools

import jax
import jax.numpy as jnp
from jax import lax
from jax.experimental import pallas as pl
from jax.experimental.pallas import tpu as pltpu
from jax.sharding import PartitionSpec as P

QD = 4
LO = 16
AXES = ("chain", "sector")


def rings(sectors):
    down = lambda k: (k // QD) * QD + (k + 1) % QD
    up = lambda k: (k + QD) % sectors
    first = [(k, down(k)) for k in range(sectors)] + [(sectors + k, sectors + up(k)) for k in range(sectors)]
    second = [(k, up(k)) for k in range(sectors)] + [(sectors + k, sectors + down(k)) for k in range(sectors)]
    swap = [(k, sectors + k) for k in range(sectors)] + [(sectors + k, k) for k in range(sectors)]
    return first, second, swap


def place():
    core, sector = lax.axis_index("chain"), lax.axis_index("sector")
    inside = lax.rem(sector, QD) < QD - 1
    from_down, from_up = lax.rem(sector, QD) > 0, sector >= QD
    return core, inside, from_down, from_up


def spread(mpo):
    w = mpo.shape[0]
    rows = lax.broadcasted_iota(jnp.int32, (w * LO, w), 0) // LO
    pick = (rows == lax.broadcasted_iota(jnp.int32, (w * LO, w), 1)).astype(jnp.bfloat16)
    tall = lax.dot_general(pick, mpo, (((1,), (1,)), ((), ())), preferred_element_type=jnp.float32).astype(jnp.bfloat16)
    full = lax.dot_general(tall, pick, (((1,), (1,)), ((), ())), preferred_element_type=jnp.float32)
    i = lax.broadcasted_iota(jnp.int32, full.shape, 0) % LO
    j = lax.broadcasted_iota(jnp.int32, full.shape, 1) % LO
    return jnp.where(i == j, full, 0.0).astype(jnp.bfloat16)


def couple(coupling, projected, column, out):
    w, blk = out.shape[0], out.shape[1]
    part = lambda a: projected[:, a:a + LO, column:column + blk].reshape(w * LO, blk)
    for a in range(0, blk, 2 * LO):
        both = jnp.concatenate([part(a), part(a + LO)], axis=1)
        mixed = jnp.dot(coupling, both, preferred_element_type=jnp.float32).astype(out.dtype)
        out[:, a:a + LO, :] = mixed[:, :blk].reshape(w, LO, blk)
        out[:, a + LO:a + 2 * LO, :] = mixed[:, blk:].reshape(w, LO, blk)


def prepare_kernel(here, other, states, states_other, local, send):
    core, inside, _, _ = place()
    middle, outer = 1 + core, 2 - core

    def block(site, state):
        same = core == site
        exists = jnp.where(same, here[state], other[state]) > 0
        kept = exists & ((state < 2) | inside)
        both = jnp.where(same, states[core, state], states_other[core, state])
        return jnp.where(kept, both, jnp.zeros_like(both))

    for site in range(2):
        local[site, 0] = block(site, middle)
        local[site, 1] = block(site, 0)
        send[site, 0] = block(site, 3)
        send[site, 1] = block(site, outer)


def own_kernel(site, env, local, mpo, mpo_other, out_q, out_r, projected):
    core, _, _, _ = place()
    right = jnp.concatenate([local[site, 0], local[site, 1]], axis=1)
    for w in range(env.shape[0]):
        projected[w] = jnp.dot(env[w], right, preferred_element_type=jnp.float32).astype(jnp.bfloat16)
    pick = lambda state: jnp.where(core == site, mpo[state], mpo_other[state])
    couple(spread(pick(1 + core)), projected, 0, out_q)
    couple(spread(pick(0)), projected, env.shape[1], out_r)


def join_kernel(site, role, env, local, sent, mpo, mpo_other, mine, out, projected, mixed):
    core, _, from_down, from_up = place()
    valid = jnp.where(core == 0, from_down, from_up)
    theirs = jnp.where(valid, sent[site, role], jnp.zeros_like(sent[site, role]))
    for w in range(env.shape[0]):
        projected[w] = jnp.dot(env[w], theirs, preferred_element_type=jnp.float32).astype(jnp.bfloat16)
    state = 3 if role == 0 else 2 - core
    couple(spread(jnp.where(core == site, mpo[state], mpo_other[state])), projected, 0, mixed)
    left = jnp.concatenate([local[site, role], theirs], axis=0)
    for v in range(env.shape[0]):
        right = jnp.concatenate([mine[v], mixed[v]], axis=0)
        out[v] = lax.dot_general(left, right, (((0,), (0,)), ((), ())), preferred_element_type=jnp.float32).astype(out.dtype)


def sum_kernel(site, rows, rows_other, kept, arrived, out):
    core, _, from_down, from_up = place()
    live = jnp.where(core == site, rows[0], rows_other[0])
    valid = jnp.where(core == 0, from_up, from_down)
    blk = out.shape[1]
    inside = (lax.broadcasted_iota(jnp.int32, (blk, blk), 0) < live) & (lax.broadcasted_iota(jnp.int32, (blk, blk), 1) < live)
    for v in range(out.shape[0]):
        total = kept[v] + jnp.where(valid, arrived[v].astype(jnp.float32), 0.0)
        out[v] = jnp.where(inside, total, 0.0).astype(out.dtype)


VMEM = pl.BlockSpec(memory_space=pltpu.VMEM)
SMEM = pl.BlockSpec(memory_space=pltpu.SMEM)


def call(kernel, out_shape, in_specs, scratch=(), flops=0, moved=1 << 20):
    single = not isinstance(out_shape, (tuple, list))
    return pl.pallas_call(
        kernel,
        out_shape=out_shape,
        in_specs=in_specs,
        out_specs=VMEM if single else [VMEM] * len(out_shape),
        scratch_shapes=scratch,
        compiler_params=pltpu.CompilerParams(vmem_limit_bytes=24 << 20),
        cost_estimate=pl.CostEstimate(flops=flops, bytes_accessed=moved, transcendentals=0),
    )


def on_device(env_first, states, mpo, block_rows, present):
    sectors = lax.axis_size("sector")
    first, second, swap = rings(sectors)
    move = lambda value, pairs: lax.ppermute(value, AXES, pairs)
    core = lax.axis_index("chain")
    _, _, width, blk, _ = env_first.shape
    env_shape = (width, blk, blk)
    half = jax.ShapeDtypeStruct(env_shape, jnp.bfloat16)
    whole = jax.ShapeDtypeStruct(env_shape, jnp.float32)

    states, mpo, rows, here = states[0, :, :, 0], mpo[0], block_rows[0], present[0, :, 0]
    states_other, mpo_other, rows_other, other = (move(x, swap) for x in (states, mpo, rows, here))
    env = lax.dynamic_index_in_dim(env_first[:, 0], core, 0, keepdims=False)
    pair = jax.ShapeDtypeStruct((2, 2, blk, blk), jnp.bfloat16)
    local, send = call(prepare_kernel, [pair, pair], [SMEM, SMEM, VMEM, VMEM])(here, other, states, states_other)
    arriving = move(env, first)
    sent = move(send, first)

    envs = []
    for site in range(2):
        mine_q, mine_r = call(
            functools.partial(own_kernel, site), [half, half], [VMEM] * 4,
            [pltpu.VMEM((width, blk, 2 * blk), jnp.bfloat16)], 1 << 29,
        )(env, local, mpo, mpo_other)
        scratch = [pltpu.VMEM(env_shape, jnp.bfloat16)] * 2
        q = call(functools.partial(join_kernel, site, 0), half, [VMEM] * 6, scratch, 1 << 29)(
            arriving, local, sent, mpo, mpo_other, mine_q)
        arrived = move(q, second)
        r = call(functools.partial(join_kernel, site, 1), whole, [VMEM] * 6, scratch, 1 << 29)(
            arriving, local, sent, mpo, mpo_other, mine_r)
        env = call(functools.partial(sum_kernel, site), half, [SMEM, SMEM, VMEM, VMEM])(rows, rows_other, r, arrived)
        envs.append(env)
        if site == 0:
            arriving = move(env, first)

    own = jnp.where(core == 0, envs[0], envs[1])
    given = jnp.where(core == 0, envs[1], envs[0])
    taken = move(given, swap)
    result = jnp.stack([jnp.where(core == 0, own, taken), jnp.where(core == 0, taken, own)])
    return result[None, :, None]


def solution(mesh):
    placed = (
        P(None, "sector", None, None, None),
        P("chain", None, None, "sector", None, None),
        P("chain", None, None, None),
        P("chain", "sector"),
        P("chain", None, "sector"),
    )
    return jax.shard_map(
        on_device,
        mesh=mesh,
        in_specs=placed,
        out_specs=P("chain", None, "sector", None, None, None),
        check_vma=False,
    )
```

```python
import functools

import jax
import jax.numpy as jnp
from jax import lax
from jax.experimental import pallas as pl
from jax.experimental.pallas import tpu as pltpu
from jax.sharding import PartitionSpec as P

QD = 4
LO = 16
AXES = ("chain", "sector")


def rings(sectors):
    down = lambda k: (k // QD) * QD + (k + 1) % QD
    up = lambda k: (k + QD) % sectors
    stay = lambda k: k

    def pairs(zero, one, cross):
        to_zero, to_one = (sectors, 0) if cross else (0, sectors)
        return [(k, to_zero + zero(k)) for k in range(sectors)] + [(sectors + k, to_one + one(k)) for k in range(sectors)]

    return pairs(down, up, False), pairs(up, down, False), pairs(up, down, True), pairs(stay, stay, True)


def place():
    core, sector = lax.axis_index("chain"), lax.axis_index("sector")
    return core, lax.rem(sector, QD) < QD - 1, lax.rem(sector, QD) > 0, sector >= QD


def target_of(site):
    core = lax.axis_index("chain")
    return core if site == 0 else 1 - core


def spreads(couplings):
    w = couplings[0].shape[0]
    rows = lax.broadcasted_iota(jnp.int32, (w * LO, w), 0) // LO
    pick = (rows == lax.broadcasted_iota(jnp.int32, (w * LO, w), 1)).astype(jnp.bfloat16)
    i = lax.broadcasted_iota(jnp.int32, (w * LO, w * LO), 0) % LO
    j = lax.broadcasted_iota(jnp.int32, (w * LO, w * LO), 1) % LO
    same = i == j

    def spread(mpo):
        tall = lax.dot_general(pick, mpo, (((1,), (1,)), ((), ())), preferred_element_type=jnp.float32).astype(jnp.bfloat16)
        full = lax.dot_general(tall, pick, (((1,), (1,)), ((), ())), preferred_element_type=jnp.float32)
        return jnp.where(same, full, 0.0).astype(jnp.bfloat16)

    return [spread(mpo) for mpo in couplings]


def couple(coupling, projected, column, out, lowest=0):
    count, blk = out.shape[0], out.shape[1]
    coupling = coupling[lowest * LO:(lowest + count) * LO]

    def part(a):
        pieces = [p[:, a:a + LO, column:column + blk].reshape(p.shape[0] * LO, blk) for p in projected]
        return pieces[0] if len(pieces) == 1 else jnp.concatenate(pieces, axis=0)

    for a in range(0, blk, 2 * LO):
        both = jnp.concatenate([part(a), part(a + LO)], axis=1)
        mixed = jnp.dot(coupling, both, preferred_element_type=jnp.float32).astype(out.dtype)
        out[:, a:a + LO, :] = mixed[:, :blk].reshape(count, LO, blk)
        out[:, a + LO:a + 2 * LO, :] = mixed[:, blk:].reshape(count, LO, blk)


def project(parts, counts, right, projected):
    slots = [(part, i) for part, count in zip(parts, counts) for i in range(count)]
    for w, (part, i) in enumerate(slots):
        projected[w] = jnp.dot(part[i], right, preferred_element_type=jnp.float32).astype(jnp.bfloat16)


def join(ours, theirs, mine, lowest, mixed, outs):
    left = jnp.concatenate([ours.T, theirs.T], axis=1)
    slots = [(out, i) for out in outs for i in range(out.shape[0])]
    blk = left.shape[0]
    for v in range(0, len(slots), 2):
        pair = range(v, min(v + 2, len(slots)))
        right = jnp.concatenate([jnp.concatenate([mine[lowest + u], mixed[u]], axis=0) for u in pair], axis=1)
        both = jnp.dot(left, right, preferred_element_type=jnp.float32)
        for n, u in enumerate(pair):
            out, i = slots[u]
            out[i] = both[:, n * blk:(n + 1) * blk].astype(out.dtype)


def prepare_kernel(here, other, rows, rows_other, states, states_other, local, send, send_later, live):
    core, inside, _, _ = place()

    def block(site, state, choice):
        same, target = core == site, target_of(site)

        def exists(k):
            flag = jnp.where(same, here[:, k:k + 1], other[:, k:k + 1]) > 0
            return flag & inside if k >= 2 else flag

        def of(k):
            both = jnp.where(same, states[target, k], states_other[target, k])
            return jnp.where(exists(k), both, jnp.zeros_like(both))

        return of(state) if state == choice else jnp.where(target == 0, of(state), of(choice))

    for site, out in enumerate((send, send_later)):
        out[0] = block(site, 3, 3)
        out[1] = block(site, 2, 1)
        local[site, 0] = block(site, 1, 2)
        local[site, 1] = block(site, 0, 0)
        live[site] = jnp.broadcast_to(jnp.where(core == site, rows[...], rows_other[...]), live.shape[1:])


def behind(site, sent):
    _, _, from_down, from_up = place()
    valid = jnp.where(target_of(site) == 0, from_down, from_up)
    return jnp.where(valid, sent, jnp.zeros_like(sent))


def own_kernel(site, counts, local, mpo, mpo_other, *refs):
    *parts, out_q, out_r, out_spread, projected = refs
    core = lax.axis_index("chain")
    right = jnp.concatenate([local[site, 0], local[site, 1]], axis=1)
    project(parts, counts, right, projected)
    pick = lambda state: jnp.where(core == site, mpo[state], mpo_other[state])
    target = target_of(site)
    middle, zero, both, outer = spreads([pick(1 + target), pick(0), pick(3), pick(2 - target)])
    couple(middle, [projected], 0, out_q)
    couple(zero, [projected], out_q.shape[1], out_r)
    out_spread[0] = both
    out_spread[1] = outer


def project_kernel(site, at, sent, part, projected):
    project([part], projected.shape[:1], behind(site, sent[at]), projected)


def head_kernel(site, at, local, sent, spread, mine, *refs):
    *projected, part, out, mine_projected, mixed = refs
    theirs = behind(site, sent[at])
    project([part], mine_projected.shape[:1], theirs, mine_projected)
    couple(spread[0], [*projected, mine_projected], 0, mixed)
    join(local[site, 0], theirs, mine, 0, mixed, [out])


def tail_kernel(site, at, local, sent, spread, mine, *refs):
    *projected, out, mixed = refs
    lowest = mine.shape[0] - out.shape[0]
    couple(spread[0], projected, 0, mixed, lowest)
    join(local[site, 0], behind(site, sent[at]), mine, lowest, mixed, [out])


def keep_kernel(site, at, counts, local, sent, spread, mine, after, *refs):
    parts, outs, (projected, mixed) = refs[:len(counts)], refs[len(counts):-2], refs[-2:]
    theirs = behind(site, sent[at + 1])
    project(parts, counts, theirs, projected)
    couple(spread[1], [projected], 0, mixed)
    join(local[site, 1], theirs, mine, 0, mixed, outs)


def total(site, live, kept, arrived, lowest, v):
    core, _, from_down, from_up = place()
    valid = jnp.where(core == 0, from_down, from_up)
    kept, at = [(part, i) for part in kept for i in range(part.shape[0])][lowest + v]
    blk = kept.shape[1]
    rows = live[site, 0:1, :]
    inside = (lax.broadcasted_iota(jnp.int32, (blk, blk), 0) < rows) & (lax.broadcasted_iota(jnp.int32, (blk, blk), 1) < rows)
    both = kept[at].astype(jnp.float32) + jnp.where(valid, arrived[v].astype(jnp.float32), 0.0)
    return jnp.where(inside, both, 0.0).astype(jnp.bfloat16)


def sum_kernel(lowest, pieces, live, arrived, *refs):
    kept, more, out = refs[:pieces], refs[pieces:-1], refs[-1]
    count = arrived.shape[0]
    for v in range(count):
        out[v] = total(0, live, kept, arrived, lowest, v)
    for blocks in more:
        for i in range(blocks.shape[0]):
            out[count + i] = blocks[i]


def last_kernel(live, arrived, kept, before, stays, given):
    core = lax.axis_index("chain")
    for v in range(stays.shape[0]):
        new, old = total(1, live, [kept], arrived, 0, v), before[v]
        stays[v] = jnp.where(core == 0, old, new)
        given[v] = jnp.where(core == 0, new, old)


def copy_all(copies, sems):
    copies = [pltpu.make_async_copy(source, target, sems.at[i]) for i, (source, target) in enumerate(copies)]
    for copy in copies:
        copy.start()
    for copy in copies:
        copy.wait()


def write_kernel(stays_head, stays_tail, taken_head, out, sems):
    core = lax.axis_index("chain")
    n, m = stays_head.shape[0], stays_tail.shape[0]
    copy_all([
        (stays_head, out.at[1 - core, pl.ds(0, n)]),
        (stays_tail, out.at[1 - core, pl.ds(n, m)]),
        (taken_head, out.at[core, pl.ds(0, n)]),
    ], sems)


def finish_kernel(begun, taken_tail, out, sems):
    core = lax.axis_index("chain")
    m = taken_tail.shape[0]
    copy_all([(taken_tail, out.at[core, pl.ds(out.shape[1] - m, m)])], sems)


VMEM = pl.BlockSpec(memory_space=pltpu.VMEM)
SMEM = pl.BlockSpec(memory_space=pltpu.SMEM)


def call(kernel, out_shape, in_specs, scratch=(), flops=0, moved=1):
    single = not isinstance(out_shape, (tuple, list))
    return pl.pallas_call(
        kernel,
        out_shape=out_shape,
        in_specs=in_specs,
        out_specs=VMEM if single else [VMEM] * len(out_shape),
        scratch_shapes=scratch,
        compiler_params=pltpu.CompilerParams(vmem_limit_bytes=24 << 20),
        cost_estimate=pl.CostEstimate(flops=1, bytes_accessed=1, transcendentals=0),
    )


def on_device(env_first, states, mpo, block_rows, present):
    sectors = lax.axis_size("sector")
    first, second, cross, swap = rings(sectors)
    move = lambda value, pairs: lax.ppermute(value, AXES, pairs)
    core = lax.axis_index("chain")
    _, _, width, blk, _ = env_first.shape
    env_shape = (width, blk, blk)
    lengths = (-(-width // 2), width // 2)
    array = lambda *shape, dtype=jnp.bfloat16: jax.ShapeDtypeStruct(shape, dtype)
    scratch = lambda n, m=1: pltpu.VMEM((n, blk, m * blk), jnp.bfloat16)
    half = array(*env_shape)
    pieces = [array(n, blk, blk) for n in lengths]
    wide = [array(n, blk, blk, dtype=jnp.float32) for n in lengths]
    small = [array(len(range(i, min(i + 5, width))), blk, blk) for i in range(0, width, 5)]

    states, mpo, rows, here = states[0, :, :, 0], mpo[0], block_rows, present[:, :, 0]
    parts = [lax.dynamic_index_in_dim(env_first[:, 0], core, 0, keepdims=False)]
    arriving = [move(part, first) for part in parts]
    states_other, mpo_other, rows_other, other = lax.optimization_barrier(tuple(move(x, swap) for x in (states, mpo, rows, here)))
    pair = array(2, blk, blk)
    local, send, send_later, live = call(
        prepare_kernel, [array(2, 2, blk, blk), pair, pair, array(2, 8, blk, dtype=jnp.int32)], [VMEM] * 6,
    )(here, other, rows, rows_other, states, states_other)
    sent = move(send, first)

    for site in range(2):
        counts, at = ((width,), 0) if site == 0 else (lengths, lengths[0])
        mine_q, mine_r, spread = call(
            functools.partial(own_kernel, site, counts), [half, half, array(2, width * LO, width * LO)], [VMEM] * (3 + len(parts)),
            [scratch(width, 2)], 1 << 29,
        )(local, mpo, mpo_other, *parts)
        projected = [
            call(functools.partial(project_kernel, site, at), array(count, blk, blk), [VMEM] * 2, (), 1 << 27)(sent, part)
            for part, count in zip(arriving[:-1], counts)
        ]
        q_head, last = call(
            functools.partial(head_kernel, site, at), [pieces[0], array(counts[-1], blk, blk)],
            [VMEM] * (5 + len(projected)), [scratch(lengths[0])], 1 << 28,
        )(local, sent, spread, mine_q, *projected, arriving[-1])
        projected.append(last)
        q_tail = call(
            functools.partial(tail_kernel, site, at), pieces[1], [VMEM] * (4 + len(projected)), [scratch(lengths[1])], 1 << 27,
        )(local, sent, spread, mine_q, *projected)
        arrived = [move(q, cross if site == 0 else first) for q in (q_head, q_tail)]
        kept = call(
            functools.partial(keep_kernel, site, at, counts), wide if site else small, [VMEM] * (5 + len(arriving)), [scratch(width)] * 2, 1 << 29,
        )(local, sent, spread, mine_r, q_tail, *arriving)
        if site == 0:
            kept = [move(part, swap) for part in kept]
            longer = array(lengths[0] + 2, blk, blk)
            parts = [
                call(functools.partial(sum_kernel, 0, len(kept)), longer, [VMEM] * (3 + len(kept)))(live, arrived[0], *kept, send_later),
                call(functools.partial(sum_kernel, lengths[0], len(kept)), pieces[1], [VMEM] * (2 + len(kept)))(live, arrived[1], *kept),
            ]
            arriving = [move(part, second) for part in parts]
            sent = arriving[0]
        else:
            both = [call(last_kernel, [pieces[i]] * 2, [VMEM] * 4)(live, arrived[i], kept[i], parts[i]) for i in range(2)]
    (stays_head, given_head), (stays_tail, given_tail) = both
    taken_head, taken_tail = move(given_head, swap), move(given_tail, swap)
    whole = array(2, *env_shape)
    hbm = pl.BlockSpec(memory_space=pl.ANY)
    params = pltpu.CompilerParams(vmem_limit_bytes=24 << 20)
    result = pl.pallas_call(
        write_kernel, out_shape=whole, in_specs=[VMEM] * 3, out_specs=hbm,
        scratch_shapes=[pltpu.SemaphoreType.DMA((3,))], compiler_params=params,
    )(stays_head, stays_tail, taken_head)
    result = pl.pallas_call(
        finish_kernel, out_shape=whole, in_specs=[hbm, VMEM], out_specs=hbm, input_output_aliases={0: 0},
        scratch_shapes=[pltpu.SemaphoreType.DMA((1,))], compiler_params=params,
    )(result, taken_tail)
    return result[None, :, None]


def solution(mesh):
    placed = (
        P(None, "sector", None, None, None),
        P("chain", None, None, "sector", None, None),
        P("chain", None, None, None),
        P("chain", "sector"),
        P("chain", None, "sector"),
    )
    return jax.shard_map(
        on_device,
        mesh=mesh,
        in_specs=placed,
        out_specs=P("chain", None, "sector", None, None, None),
        check_vma=False,
    )
```

```python
import functools

import jax
import jax.numpy as jnp
from jax import lax
from jax.experimental import pallas as pl
from jax.experimental.pallas import tpu as pltpu
from jax.sharding import PartitionSpec as P

QD = 4
LO = 16
AXES = ("chain", "sector")


def rings(sectors):
    down = lambda k: (k // QD) * QD + (k + 1) % QD
    up = lambda k: (k + QD) % sectors
    stay = lambda k: k

    def pairs(zero, one, cross):
        to_zero, to_one = (sectors, 0) if cross else (0, sectors)
        return [(k, to_zero + zero(k)) for k in range(sectors)] + [(sectors + k, to_one + one(k)) for k in range(sectors)]

    last = sectors - QD
    column = [(sectors + k, sectors + k + QD if k < last else k) for k in range(sectors)]
    column += [(k, k - QD if k >= QD else sectors + k) for k in range(sectors)]
    return {
        "envs": pairs(down, up, False),
        "partials": pairs(up, down, True),
        "new_envs": pairs(up, down, False),
        "up": column,
        "down": pairs(down, stay, True),
        "swap": pairs(stay, stay, True),
    }


def place():
    core, sector = lax.axis_index("chain"), lax.axis_index("sector")
    return core, lax.rem(sector, QD) < QD - 1, lax.rem(sector, QD) > 0, sector >= QD


def spreads(couplings):
    w = couplings[0].shape[0]
    rows = lax.broadcasted_iota(jnp.int32, (w * LO, w), 0) // LO
    pick = (rows == lax.broadcasted_iota(jnp.int32, (w * LO, w), 1)).astype(jnp.bfloat16)
    i = lax.broadcasted_iota(jnp.int32, (w * LO, w * LO), 0) % LO
    j = lax.broadcasted_iota(jnp.int32, (w * LO, w * LO), 1) % LO
    same = i == j

    def spread(mpo):
        tall = lax.dot_general(pick, mpo, (((1,), (1,)), ((), ())), preferred_element_type=jnp.float32).astype(jnp.bfloat16)
        full = lax.dot_general(tall, pick, (((1,), (1,)), ((), ())), preferred_element_type=jnp.float32)
        return jnp.where(same, full, 0.0).astype(jnp.bfloat16)

    return [spread(mpo) for mpo in couplings]


def couple(coupling, projected, column, out, lowest=0):
    count, blk = out.shape[0], out.shape[1]
    coupling = coupling[lowest * LO:(lowest + count) * LO]

    def part(a):
        pieces = [p[:, a:a + LO, column:column + blk].reshape(p.shape[0] * LO, blk) for p in projected]
        return pieces[0] if len(pieces) == 1 else jnp.concatenate(pieces, axis=0)

    for a in range(0, blk, 2 * LO):
        both = jnp.concatenate([part(a), part(a + LO)], axis=1)
        mixed = jnp.dot(coupling, both, preferred_element_type=jnp.float32).astype(out.dtype)
        out[:, a:a + LO, :] = mixed[:, :blk].reshape(count, LO, blk)
        out[:, a + LO:a + 2 * LO, :] = mixed[:, blk:].reshape(count, LO, blk)


def project(parts, counts, right, projected):
    slots = [(part, i) for part, count in zip(parts, counts) for i in range(count)]
    for w, (part, i) in enumerate(slots):
        projected[w] = jnp.dot(part[i], right, preferred_element_type=jnp.float32).astype(jnp.bfloat16)


def join(ours, theirs, mine, lowest, mixed, outs):
    left = jnp.concatenate([ours.T, theirs.T], axis=1)
    slots = [(out, i) for out in outs for i in range(out.shape[0])]
    blk = left.shape[0]
    for v in range(0, len(slots), 2):
        pair = range(v, min(v + 2, len(slots)))
        right = jnp.concatenate([jnp.concatenate([mine[lowest + u], mixed[u]], axis=0) for u in pair], axis=1)
        both = jnp.dot(left, right, preferred_element_type=jnp.float32)
        for n, u in enumerate(pair):
            out, i = slots[u]
            out[i] = both[:, n * blk:(n + 1) * blk].astype(out.dtype)


def prepare_kernel(here, other, rows, rows_other, states, states_other, local, send, later, live):
    core, inside, _, _ = place()

    def block(site, target, state, choice):
        same = core == site

        def exists(k):
            flag = jnp.where(same, here[:, k:k + 1], other[:, k:k + 1]) > 0
            return flag & inside if k >= 2 else flag

        def of(k):
            both = jnp.where(same, states[target, k], states_other[target, k])
            return jnp.where(exists(k), both, jnp.zeros_like(both))

        return of(state) if state == choice else jnp.where(target == 0, of(state), of(choice))

    send[0] = block(0, core, 3, 3)
    local[0, 0] = block(0, core, 1, 2)
    local[0, 1] = block(0, core, 0, 0)
    local[1, 0] = block(1, 1 - core, 1, 2)
    local[1, 1] = block(1, 1 - core, 0, 0)
    send[1] = block(0, core, 2, 1)
    later[0] = block(1, 1 - core, 3, 3)
    later[1] = block(1, 1 - core, 2, 1)
    for site in range(2):
        live[site] = jnp.broadcast_to(jnp.where(core == site, rows[...], rows_other[...]), live.shape[1:])


def behind(target, sent):
    _, _, from_down, from_up = place()
    return jnp.where(jnp.where(target == 0, from_down, from_up), sent, jnp.zeros_like(sent))


def own_kernel(site, counts, local, mpo, mpo_other, *refs):
    *parts, out_q, out_r, out_spread, projected = refs
    core, target = lax.axis_index("chain"), target_of(site)
    pick = lambda state: jnp.where(core == site, mpo[state], mpo_other[state])
    middle, zero, both, outer = spreads([pick(1 + target), pick(0), pick(3), pick(2 - target)])
    project(parts, counts, jnp.concatenate([local[site, 0], local[site, 1]], axis=1), projected)
    couple(middle, [projected], 0, out_q)
    couple(zero, [projected], out_q.shape[1], out_r)
    out_spread[0] = both
    out_spread[1] = outer


def target_of(site):
    core = lax.axis_index("chain")
    return core if site == 0 else 1 - core


def project_kernel(site, at, sent, part, projected):
    project([part], projected.shape[:1], behind(target_of(site), sent[at]), projected)


def head_kernel(site, at, local, sent, spread, mine, *refs):
    *projected, part, out, mine_projected, mixed = refs
    theirs = behind(target_of(site), sent[at])
    project([part], mine_projected.shape[:1], theirs, mine_projected)
    couple(spread[0], [*projected, mine_projected], 0, mixed)
    join(local[site, 0], theirs, mine, 0, mixed, [out])


def tail_kernel(site, at, local, sent, spread, mine, *refs):
    *projected, out, mixed = refs
    lowest = mine.shape[0] - out.shape[0]
    couple(spread[0], projected, 0, mixed, lowest)
    join(local[site, 0], behind(target_of(site), sent[at]), mine, lowest, mixed, [out])


def keep_kernel(site, at, counts, local, sent, spread, mine, after, *refs):
    parts, refs = refs[:len(counts)], refs[len(counts):]
    theirs = behind(target_of(site), sent[at + 1])
    *outs, projected, mixed = refs
    project(parts, counts, theirs, projected)
    couple(spread[1], [projected], 0, mixed)
    join(local[site, 1], theirs, mine, 0, mixed, outs)


def give_kernel(pieces, *refs):
    kept, envs, outs = refs[:pieces], refs[pieces:2 * pieces], refs[2 * pieces:]
    core = lax.axis_index("chain")
    blocks = [(a, b, i) for a, b in zip(kept, envs) for i in range(a.shape[0])]
    slots = [(out, i) for out in outs for i in range(out.shape[0])]
    for (a, b, i), (out, j) in zip(blocks, slots):
        out[j] = jnp.where(core == 0, a[i].astype(jnp.bfloat16), b[i])


def total(site, live, valid, kept, arrived):
    blk = kept.shape[0]
    rows = live[site, 0:1, :]
    inside = (lax.broadcasted_iota(jnp.int32, (blk, blk), 0) < rows) & (lax.broadcasted_iota(jnp.int32, (blk, blk), 1) < rows)
    both = kept.astype(jnp.float32) + jnp.where(valid, arrived.astype(jnp.float32), 0.0)
    return jnp.where(inside, both, 0.0).astype(jnp.bfloat16)


def sum_kernel(lowest, pieces, live, arrived, *refs):
    kept, more, out = refs[:pieces], refs[pieces:-1], refs[-1]
    core, _, from_down, from_up = place()
    valid = jnp.where(core == 0, from_down, from_up)
    slots = [(part, i) for part in kept for i in range(part.shape[0])]
    count = arrived.shape[0]
    for v in range(count):
        part, i = slots[lowest + v]
        out[v] = total(0, live, valid, part[i], arrived[v])
    for blocks in more:
        for i in range(blocks.shape[0]):
            out[count + i] = blocks[i]


def last_kernel(lowest, pieces, started, live, from_up_arrived, from_down_arrived, kept, env, *refs):
    taken, refs = refs[:pieces], refs[pieces + started:]
    out, new, sems = refs
    core, _, from_down, from_up = place()
    count = kept.shape[0]
    slots = [(part, i) for part in taken for i in range(part.shape[0])][lowest:lowest + count]
    for v in range(count):
        part, i = slots[v]
        received = part[i]
        new[0, v] = jnp.where(core == 0, received, total(1, live, from_up, kept[v], from_up_arrived[v]))
        new[1, v] = jnp.where(core == 0, env[v], total(1, live, from_down, received, from_down_arrived[v]))
    copy_all([(new.at[t], out.at[t, pl.ds(lowest, count)]) for t in range(2)], sems)


def copy_all(copies, sems):
    copies = [pltpu.make_async_copy(source, target, sems.at[i]) for i, (source, target) in enumerate(copies)]
    for copy in copies:
        copy.start()
    for copy in copies:
        copy.wait()


VMEM = pl.BlockSpec(memory_space=pltpu.VMEM)
SMEM = pl.BlockSpec(memory_space=pltpu.SMEM)


def call(kernel, out_shape, in_specs, scratch=()):
    single = not isinstance(out_shape, (tuple, list))
    return pl.pallas_call(
        kernel,
        out_shape=out_shape,
        in_specs=in_specs,
        out_specs=VMEM if single else [VMEM] * len(out_shape),
        scratch_shapes=scratch,
        compiler_params=pltpu.CompilerParams(vmem_limit_bytes=24 << 20),
        cost_estimate=pl.CostEstimate(flops=1, bytes_accessed=1, transcendentals=0),
    )


def on_device(env_first, states, mpo, block_rows, present):
    pairs = rings(lax.axis_size("sector"))
    move = lambda value, name: lax.ppermute(value, AXES, pairs[name])
    core = lax.axis_index("chain")
    _, _, width, blk, _ = env_first.shape
    lengths = (-(-width // 2), width // 2)
    lowest = (0, lengths[0])
    array = lambda *shape, dtype=jnp.bfloat16: jax.ShapeDtypeStruct(shape, dtype)
    scratch = lambda n, m=1: pltpu.VMEM((n, blk, m * blk), jnp.bfloat16)
    half = array(width, blk, blk)
    spread_shape = array(2, width * LO, width * LO)
    pieces = [array(n, blk, blk) for n in lengths]
    wide = [array(n, blk, blk, dtype=jnp.float32) for n in lengths]
    small = [array(len(range(i, min(i + 5, width))), blk, blk) for i in range(0, width, 5)]

    env_first = env_first[:, 0]
    states, mpo, rows, here = states[0, :, :, 0], mpo[0], block_rows, present[:, :, 0]
    env = lax.dynamic_index_in_dim(env_first, core, 0, keepdims=False)
    arriving = move(env, "envs")
    states_other, mpo_other, rows_other, other = lax.optimization_barrier(tuple(move(x, "swap") for x in (states, mpo, rows, here)))
    local, send, later, live = call(
        prepare_kernel, [array(2, 2, blk, blk), array(2, blk, blk), array(2, blk, blk), array(2, 8, blk, dtype=jnp.int32)], [VMEM] * 6,
    )(here, other, rows, rows_other, states, states_other)
    sent = move(send, "envs")

    own = lambda site, counts: call(
        functools.partial(own_kernel, site, counts), [half, half, spread_shape], [VMEM] * (3 + len(counts)), [scratch(width, 2)])
    mine_q, mine_r, spread = own(0, (width,))(local, mpo, mpo_other, env)
    q_head, projected = call(functools.partial(head_kernel, 0, 0), [pieces[0], half], [VMEM] * 5, [scratch(lengths[0])])(
        local, sent, spread, mine_q, arriving)
    q_tail = call(functools.partial(tail_kernel, 0, 0), pieces[1], [VMEM] * 5, [scratch(lengths[1])])(
        local, sent, spread, mine_q, projected)
    arrived = [move(q, "partials") for q in (q_head, q_tail)]
    kept = call(functools.partial(keep_kernel, 0, 0, (width,)), small, [VMEM] * 6, [scratch(width)] * 2)(
        local, sent, spread, mine_r, q_tail, arriving)
    kept = [move(part, "swap") for part in kept]
    with_blocks = array(lengths[0] + 2, blk, blk)
    envs = [
        call(functools.partial(sum_kernel, lowest[0], len(kept)), with_blocks, [VMEM] * (3 + len(kept)))(live, arrived[0], *kept, later),
        call(functools.partial(sum_kernel, lowest[1], len(kept)), pieces[1], [VMEM] * (2 + len(kept)))(live, arrived[1], *kept),
    ]
    arriving = [move(env, "new_envs") for env in envs]
    sent, at = arriving[0], lengths[0]

    mine_q, mine_r, spread = own(1, lengths)(local, mpo, mpo_other, *envs)
    early = call(functools.partial(project_kernel, 1, at), pieces[0], [VMEM] * 2)(sent, arriving[0])
    q_head, projected = call(functools.partial(head_kernel, 1, at), pieces, [VMEM] * 6, [scratch(lengths[0])])(
        local, sent, spread, mine_q, early, arriving[1])
    q_tail = call(functools.partial(tail_kernel, 1, at), pieces[1], [VMEM] * 6, [scratch(lengths[1])])(
        local, sent, spread, mine_q, early, projected)
    downs = [move(q, "down") for q in (q_head, q_tail)]
    ups = [move(q, "up") for q in (q_head, q_tail)]
    kept = call(functools.partial(keep_kernel, 1, at, lengths), wide, [VMEM] * 7, [scratch(width)] * 2)(
        local, sent, spread, mine_r, q_tail, *arriving)
    given = call(functools.partial(give_kernel, 2), small, [VMEM] * 4)(*kept, *envs)
    taken = [move(part, "swap") for part in lax.optimization_barrier((given, downs[0]))[0]]
    hbm = pl.BlockSpec(memory_space=pl.ANY)
    result = []
    for i in range(2):
        result = [pl.pallas_call(
            functools.partial(last_kernel, lowest[i], len(taken), i),
            out_shape=array(2, width, blk, blk),
            in_specs=[VMEM] * (5 + len(taken)) + [hbm] * i,
            out_specs=hbm,
            scratch_shapes=[pltpu.VMEM((2, lengths[i], blk, blk), jnp.bfloat16), pltpu.SemaphoreType.DMA((2,))],
            input_output_aliases={5 + len(taken): 0} if i else {},
            compiler_params=pltpu.CompilerParams(vmem_limit_bytes=24 << 20),
            cost_estimate=pl.CostEstimate(flops=1, bytes_accessed=1, transcendentals=0),
        )(live, ups[i], downs[i], kept[i], envs[i], *taken, *result)]
    return result[0][None, :, None]


def solution(mesh):
    placed = (
        P(None, "sector", None, None, None),
        P("chain", None, None, "sector", None, None),
        P("chain", None, None, None),
        P("chain", "sector"),
        P("chain", None, "sector"),
    )
    return jax.shard_map(
        on_device,
        mesh=mesh,
        in_specs=placed,
        out_specs=P("chain", None, "sector", None, None, None),
        check_vma=False,
    )
```

```python
import functools

import jax
import jax.numpy as jnp
from jax import lax
from jax.experimental import pallas as pl
from jax.experimental.pallas import tpu as pltpu
from jax.sharding import PartitionSpec as P

QD = 4
LO = 16
AXES = ("chain", "sector")
BC = (7, 8)
EE = (8, 7)
DD = (7, 8)
GG = (5, 5, 5)
ACROSS = [(4, 5), (5, 6), (6, 7), (7, 1), (1, 3), (3, 2), (2, 0), (0, 4)]


def cut(width, shares):
    ends = [round(width * sum(shares[:i]) / sum(shares)) for i in range(len(shares) + 1)]
    return tuple(b - a for a, b in zip(ends, ends[1:]))


def rings(sectors):
    down = lambda k: (k // QD) * QD + (k + 1) % QD
    up = lambda k: (k + QD) % sectors
    stay = lambda k: k

    def pairs(zero, one, cross):
        to_zero, to_one = (sectors, 0) if cross else (0, sectors)
        return [(k, to_zero + zero(k)) for k in range(sectors)] + [(sectors + k, to_one + one(k)) for k in range(sectors)]

    last = sectors - QD
    column = [(sectors + k, sectors + k + QD if k < last else k) for k in range(sectors)]
    column += [(k, k - QD if k >= QD else sectors + k) for k in range(sectors)]
    lift = [(k, k + QD if k < last else sectors + k) for k in range(sectors)]
    lift += [(sectors + k, sectors + k - QD if k >= QD else k) for k in range(sectors)]
    across = [(a // QD * sectors + g + a % QD, b // QD * sectors + g + b % QD) for g in range(0, sectors, QD) for a, b in ACROSS]

    return {
        "lift": lift,
        "across": across,
        "envs": pairs(down, up, True),
        "partials": pairs(down, up, False),
        "up": column,
        "down": pairs(down, stay, True),
        "swap": pairs(stay, stay, True),
    }


def place():
    core, sector = lax.axis_index("chain"), lax.axis_index("sector")
    return core, lax.rem(sector, QD) < QD - 1, lax.rem(sector, QD) > 0, sector >= QD


def spreads(couplings):
    w = couplings[0].shape[0]
    rows = lax.broadcasted_iota(jnp.int32, (w * LO, w), 0) // LO
    pick = (rows == lax.broadcasted_iota(jnp.int32, (w * LO, w), 1)).astype(jnp.bfloat16)
    i = lax.broadcasted_iota(jnp.int32, (w * LO, w * LO), 0) % LO
    j = lax.broadcasted_iota(jnp.int32, (w * LO, w * LO), 1) % LO
    same = i == j

    def spread(mpo):
        tall = lax.dot_general(pick, mpo, (((1,), (1,)), ((), ())), preferred_element_type=jnp.float32).astype(jnp.bfloat16)
        full = lax.dot_general(tall, pick, (((1,), (1,)), ((), ())), preferred_element_type=jnp.float32)
        return jnp.where(same, full, 0.0).astype(jnp.bfloat16)

    return [spread(mpo) for mpo in couplings]


def couple(coupling, projected, column, out, lowest=0):
    count, blk = out.shape[0], out.shape[1]
    coupling = coupling[lowest * LO:(lowest + count) * LO]

    def part(a):
        pieces = [p[:, a:a + LO, column:column + blk].reshape(p.shape[0] * LO, blk) for p in projected]
        return pieces[0] if len(pieces) == 1 else jnp.concatenate(pieces, axis=0)

    for a in range(0, blk, 2 * LO):
        both = jnp.concatenate([part(a), part(a + LO)], axis=1)
        mixed = jnp.dot(coupling, both, preferred_element_type=jnp.float32).astype(out.dtype)
        out[:, a:a + LO, :] = mixed[:, :blk].reshape(count, LO, blk)
        out[:, a + LO:a + 2 * LO, :] = mixed[:, blk:].reshape(count, LO, blk)


def project(parts, counts, right, projected):
    slots = [(part, i) for part, count in zip(parts, counts) for i in range(count)]
    for w, (part, i) in enumerate(slots):
        projected[w] = jnp.dot(part[i], right, preferred_element_type=jnp.float32).astype(jnp.bfloat16)


def join(ours, theirs, mine, lowest, mixed, outs):
    left = jnp.concatenate([ours.T, theirs.T], axis=1)
    slots = [(out, i) for out in outs for i in range(out.shape[0])]
    blk = left.shape[0]
    for v in range(0, len(slots), 2):
        pair = range(v, min(v + 2, len(slots)))
        right = jnp.concatenate([jnp.concatenate([mine[lowest + u], mixed[u]], axis=0) for u in pair], axis=1)
        both = jnp.dot(left, right, preferred_element_type=jnp.float32)
        for n, u in enumerate(pair):
            out, i = slots[u]
            out[i] = both[:, n * blk:(n + 1) * blk].astype(out.dtype)


def prepare_kernel(here, other, rows, rows_other, states, states_other, local, send, later, live):
    core, inside, _, _ = place()

    def block(site, target, state, choice):
        same = core == site

        def exists(k):
            flag = jnp.where(same, here[:, k:k + 1], other[:, k:k + 1]) > 0
            return flag & inside if k >= 2 else flag

        def of(k):
            both = jnp.where(same, states[target, k], states_other[target, k])
            return jnp.where(exists(k), both, jnp.zeros_like(both))

        return of(state) if state == choice else jnp.where(target == 0, of(state), of(choice))

    send[0] = block(0, core, 3, 3)
    local[0, 0] = block(0, 1 - core, 1, 2)
    local[0, 1] = block(0, 1 - core, 0, 0)
    local[1, 0] = block(1, 1 - core, 1, 2)
    local[1, 1] = block(1, 1 - core, 0, 0)
    send[1] = block(0, core, 2, 1)
    later[0] = block(1, 1 - core, 3, 3)
    later[1] = block(1, 1 - core, 2, 1)
    for site in range(2):
        live[site] = jnp.broadcast_to(jnp.where(core == site, rows[...], rows_other[...]), live.shape[1:])


def behind(sent):
    core, _, from_down, from_up = place()
    return jnp.where(jnp.where(core == 1, from_down, from_up), sent, jnp.zeros_like(sent))


def own_kernel(site, counts, local, mpo, mpo_other, *refs):
    *parts, out_q, out_r, out_spread, projected = refs
    core = lax.axis_index("chain")
    pick = lambda state: jnp.where(core == site, mpo[state], mpo_other[state])
    middle, zero, both, outer = spreads([pick(2 - core), pick(0), pick(3), pick(1 + core)])
    project(parts, counts, jnp.concatenate([local[site, 0], local[site, 1]], axis=1), projected)
    couple(middle, [projected], 0, out_q)
    couple(zero, [projected], out_q.shape[1], out_r)
    out_spread[0] = both
    out_spread[1] = outer


def project_kernel(site, at, sent, part, projected):
    project([part], projected.shape[:1], behind(sent[at]), projected)


def head_kernel(site, at, local, sent, spread, mine, *refs):
    *projected, part, out, mine_projected, mixed = refs
    theirs = behind(sent[at])
    project([part], mine_projected.shape[:1], theirs, mine_projected)
    couple(spread[0], [*projected, mine_projected], 0, mixed)
    join(local[site, 0], theirs, mine, 0, mixed, [out])


def tail_kernel(site, at, lowest, pieces, local, sent, spread, mine, *refs):
    projected, out, mixed = refs[:pieces], refs[-2], refs[-1]
    couple(spread[0], projected, 0, mixed, lowest)
    join(local[site, 0], behind(sent[at]), mine, lowest, mixed, [out])


def keep_kernel(site, at, counts, local, sent, spread, mine, after, *refs):
    parts, refs = refs[:len(counts)], refs[len(counts):]
    *outs, projected, mixed = refs
    theirs = behind(sent[at + 1])
    project(parts, counts, theirs, projected)
    couple(spread[1], [projected], 0, mixed)
    join(local[site, 1], theirs, mine, 0, mixed, outs)


def give_kernel(parts, kept, *refs):
    envs, outs = refs[:parts], refs[parts:]
    core, width = lax.axis_index("chain"), kept.shape[0]
    for v, ((env, i), (out, j)) in enumerate(zip(blocks_of(envs, width), blocks_of(outs, width))):
        out[j] = jnp.where(core == 0, kept[v].astype(jnp.bfloat16), env[i])


def blocks_of(parts, width):
    extra = sum(part.shape[0] for part in parts) - width
    return [(part, i) for n, part in enumerate(parts) for i in range(part.shape[0] - (0 if n else extra))]


def total(site, live, valid, kept, arrived):
    blk = kept.shape[0]
    rows = live[site, 0:1, :]
    inside = (lax.broadcasted_iota(jnp.int32, (blk, blk), 0) < rows) & (lax.broadcasted_iota(jnp.int32, (blk, blk), 1) < rows)
    both = kept.astype(jnp.float32) + jnp.where(valid, arrived.astype(jnp.float32), 0.0)
    return jnp.where(inside, both, 0.0).astype(jnp.bfloat16)


def sum_kernel(lowest, live, arrived, kept, *refs):
    more, out = refs[0], refs[-1]
    core, _, from_down, from_up = place()
    valid = jnp.where(core == 0, from_down, from_up)
    count = arrived.shape[0]
    for v in range(count):
        out[v] = total(0, live, valid, kept[lowest + v], arrived[v])
    for i in range(out.shape[0] - count):
        out[count + i] = more[i]


def pick_kernel(from_down, from_up, out):
    core = lax.axis_index("chain")
    for i in range(out.shape[0]):
        out[i] = jnp.where(core == 0, from_up[i], from_down[i])


def last_kernel(lowest, parts, started, live, from_up_arrived, from_down_arrived, kept, *refs):
    *refs, out, new, sems = refs
    taken, envs = refs[:parts], refs[parts + started:]
    core, _, from_down, from_up = place()
    count, width = from_up_arrived.shape[0], kept.shape[0]
    received = [part[i] for part, i in blocks_of(taken, width)[lowest:lowest + count]]
    slots = blocks_of(envs, width)[lowest:lowest + count]
    copies = [pltpu.make_async_copy(new.at[t], out.at[t, pl.ds(lowest, count)], sems.at[t]) for t in range(2)]
    for v in range(count):
        here = total(1, live, from_up, kept[lowest + v], from_up_arrived[v])
        new[0, v] = jnp.where(core == 0, received[v], here)
    copies[0].start()
    for v, (env, i) in enumerate(slots):
        here = total(1, live, from_down, received[v], from_down_arrived[v])
        new[1, v] = jnp.where(core == 0, env[i], here)
    copies[1].start()
    for copy in copies:
        copy.wait()


VMEM = pl.BlockSpec(memory_space=pltpu.VMEM)
SMEM = pl.BlockSpec(memory_space=pltpu.SMEM)


def call(kernel, out_shape, in_specs, scratch=()):
    single = not isinstance(out_shape, (tuple, list))
    return pl.pallas_call(
        kernel,
        out_shape=out_shape,
        in_specs=in_specs,
        out_specs=VMEM if single else [VMEM] * len(out_shape),
        scratch_shapes=scratch,
        compiler_params=pltpu.CompilerParams(vmem_limit_bytes=24 << 20),
        cost_estimate=pl.CostEstimate(flops=1, bytes_accessed=1, transcendentals=0),
    )


def on_device(env_first, states, mpo, block_rows, present):
    pairs = rings(lax.axis_size("sector"))
    move = lambda value, name: lax.ppermute(value, AXES, pairs[name])
    core = lax.axis_index("chain")
    _, _, width, blk, _ = env_first.shape
    array = lambda *shape, dtype=jnp.bfloat16: jax.ShapeDtypeStruct(shape, dtype)
    blocks = lambda n, dtype=jnp.bfloat16: array(n, blk, blk, dtype=dtype)
    scratch = lambda n, m=1: pltpu.VMEM((n, blk, m * blk), jnp.bfloat16)
    half = blocks(width)
    spread_shape = array(2, width * LO, width * LO)
    lengths = cut(width, BC)
    ends = cut(width, DD)
    starts = lambda counts: [sum(counts[:i]) for i in range(len(counts))]

    env_first = env_first[:, 0]
    states, mpo, rows, here = states[0, :, :, 0], mpo[0], block_rows, present[:, :, 0]
    env = lax.dynamic_index_in_dim(env_first, core, 0, keepdims=False)
    arriving = move(env, "envs")
    states_other, mpo_other, rows_other, other = lax.optimization_barrier(tuple(move(x, "swap") for x in (states, mpo, rows, here)))
    local, send, later, live = call(
        prepare_kernel, [array(2, 2, blk, blk), array(2, blk, blk), array(2, blk, blk), array(2, 8, blk, dtype=jnp.int32)], [VMEM] * 6,
    )(here, other, rows, rows_other, states, states_other)
    sent = move(send, "envs")
    env = lax.optimization_barrier((env, local))[0]
    given = cut(width, EE)
    env = [move(env[low:low + n], "swap") for low, n in zip(starts(given), given)]

    own = lambda site, counts: call(
        functools.partial(own_kernel, site, counts), [half, half, spread_shape], [VMEM] * (3 + len(counts)), [scratch(width, 2)])

    def outgoing(site, at, sent, spread, mine, projected, part, count, counts):
        fixed = (local, sent, spread, mine)
        first, last = call(
            functools.partial(head_kernel, site, at), [blocks(counts[0]), blocks(count)], [VMEM] * (5 + len(projected)), [scratch(counts[0])],
        )(*fixed, *projected, part)
        projected = [*projected, last]
        out = [first]
        for low, n in list(zip(starts(counts), counts))[1:]:
            out.append(call(
                functools.partial(tail_kernel, site, at, low, len(projected)), blocks(n), [VMEM] * (4 + len(projected) + len(out)), [scratch(n)],
            )(*fixed, *projected, *out))
        return out

    mine_q, mine_r, spread = own(0, given)(local, mpo, mpo_other, *env)
    q = outgoing(0, 0, sent, spread, mine_q, [], arriving, width, lengths)
    arrived = [move(part, "partials") for part in q]
    whole = blocks(width, jnp.float32)
    kept = call(functools.partial(keep_kernel, 0, 0, (width,)), whole, [VMEM] * 6, [scratch(width)] * 2)(
        local, sent, spread, mine_r, q[-1], arriving)
    envs = []
    for low, n, part in zip(starts(lengths), lengths, arrived):
        extra = 0 if envs else later.shape[0]
        envs.append(call(functools.partial(sum_kernel, low), blocks(n + extra), [VMEM] * (4 + len(envs)))(live, part, kept, later, *envs))
    arriving = [
        call(pick_kernel, blocks(env.shape[0]), [VMEM] * 2)(move(env, "across"), move(env, "lift")) for env in envs
    ]
    sent, at = arriving[0], lengths[0]

    mine_q, mine_r, spread = own(1, lengths)(local, mpo, mpo_other, *envs)
    early = [
        call(functools.partial(project_kernel, 1, at), blocks(n), [VMEM] * 2)(sent, part) for part, n in zip(arriving[:-1], lengths)
    ]
    q = outgoing(1, at, sent, spread, mine_q, early, arriving[-1], lengths[-1], ends)
    downs = [move(part, "down") for part in q]
    ups = [move(part, "up") for part in q]
    kept = call(functools.partial(keep_kernel, 1, at, lengths), whole, [VMEM] * (5 + len(arriving)), [scratch(width)] * 2)(
        local, sent, spread, mine_r, q[-1], *arriving)
    given = call(functools.partial(give_kernel, len(envs)), [blocks(n) for n in cut(width, GG)], [VMEM] * (1 + len(envs)))(kept, *envs)
    taken = [move(part, "swap") for part in lax.optimization_barrier((given, downs[0]))[0]]
    hbm = pl.BlockSpec(memory_space=pl.ANY)
    result = []
    for i, low in enumerate(starts(ends)):
        result = [pl.pallas_call(
            functools.partial(last_kernel, low, len(taken), len(result)),
            out_shape=array(2, width, blk, blk),
            in_specs=[VMEM] * (4 + len(taken)) + [hbm] * len(result) + [VMEM] * len(envs),
            out_specs=hbm,
            scratch_shapes=[pltpu.VMEM((2, ends[i], blk, blk), jnp.bfloat16), pltpu.SemaphoreType.DMA((2,))],
            input_output_aliases={4 + len(taken): 0} if result else {},
            compiler_params=pltpu.CompilerParams(vmem_limit_bytes=24 << 20),
            cost_estimate=pl.CostEstimate(flops=1, bytes_accessed=1, transcendentals=0),
        )(live, ups[i], downs[i], kept, *taken, *result, *envs)]
    return result[0][None, :, None]


def solution(mesh):
    placed = (
        P(None, "sector", None, None, None),
        P("chain", None, None, "sector", None, None),
        P("chain", None, None, None),
        P("chain", "sector"),
        P("chain", None, "sector"),
    )
    return jax.shard_map(
        on_device,
        mesh=mesh,
        in_specs=placed,
        out_specs=P("chain", None, "sector", None, None, None),
        check_vma=False,
    )
```

```python
import functools

import jax
import jax.numpy as jnp
from jax import lax
from jax.experimental import pallas as pl
from jax.experimental.pallas import tpu as pltpu
from jax.sharding import PartitionSpec as P

QD = 4
LO = 16
AXES = ("chain", "sector")
BC = (7, 8)
EE = (8, 7)
DD = (7, 8)
STEP = 3
GG = (5, 5, 5)
ACROSS = [(4, 5), (5, 6), (6, 7), (7, 1), (1, 3), (3, 2), (2, 0), (0, 4)]


def cut(width, shares):
    ends = [round(width * sum(shares[:i]) / sum(shares)) for i in range(len(shares) + 1)]
    return tuple(b - a for a, b in zip(ends, ends[1:]))


def rings(sectors):
    down = lambda k: (k // QD) * QD + (k + 1) % QD
    up = lambda k: (k + QD) % sectors
    stay = lambda k: k

    def pairs(zero, one, cross):
        to_zero, to_one = (sectors, 0) if cross else (0, sectors)
        return [(k, to_zero + zero(k)) for k in range(sectors)] + [(sectors + k, to_one + one(k)) for k in range(sectors)]

    last = sectors - QD
    column = [(sectors + k, sectors + k + QD if k < last else k) for k in range(sectors)]
    column += [(k, k - QD if k >= QD else sectors + k) for k in range(sectors)]
    lift = [(k, k + QD if k < last else sectors + k) for k in range(sectors)]
    lift += [(sectors + k, sectors + k - QD if k >= QD else k) for k in range(sectors)]
    across = [(a // QD * sectors + g + a % QD, b // QD * sectors + g + b % QD) for g in range(0, sectors, QD) for a, b in ACROSS]

    return {
        "lift": lift,
        "across": across,
        "envs": pairs(down, up, True),
        "partials": pairs(down, up, False),
        "up": column,
        "down": pairs(down, stay, True),
        "swap": pairs(stay, stay, True),
    }


def place():
    core, sector = lax.axis_index("chain"), lax.axis_index("sector")
    return core, lax.rem(sector, QD) < QD - 1, lax.rem(sector, QD) > 0, sector >= QD


def spreads(couplings):
    w = couplings[0].shape[0]
    rows = lax.broadcasted_iota(jnp.int32, (w * LO, w), 0) // LO
    pick = (rows == lax.broadcasted_iota(jnp.int32, (w * LO, w), 1)).astype(jnp.bfloat16)
    i = lax.broadcasted_iota(jnp.int32, (w * LO, w * LO), 0) % LO
    j = lax.broadcasted_iota(jnp.int32, (w * LO, w * LO), 1) % LO
    same = i == j

    def spread(mpo):
        tall = lax.dot_general(pick, mpo, (((1,), (1,)), ((), ())), preferred_element_type=jnp.float32).astype(jnp.bfloat16)
        full = lax.dot_general(tall, pick, (((1,), (1,)), ((), ())), preferred_element_type=jnp.float32)
        return jnp.where(same, full, 0.0).astype(jnp.bfloat16)

    return [spread(mpo) for mpo in couplings]


def couple(coupling, projected, column, out, lowest=0):
    count, blk = out.shape[0], out.shape[1]
    coupling = coupling[lowest * LO:(lowest + count) * LO]

    def part(a):
        pieces = [p[:, a:a + LO, column:column + blk].reshape(p.shape[0] * LO, blk) for p in projected]
        return pieces[0] if len(pieces) == 1 else jnp.concatenate(pieces, axis=0)

    for a in range(0, blk, 2 * LO):
        both = jnp.concatenate([part(a), part(a + LO)], axis=1)
        mixed = jnp.dot(coupling, both, preferred_element_type=jnp.float32).astype(out.dtype)
        out[:, a:a + LO, :] = mixed[:, :blk].reshape(count, LO, blk)
        out[:, a + LO:a + 2 * LO, :] = mixed[:, blk:].reshape(count, LO, blk)


def project(parts, counts, right, projected):
    slots = [(part, i) for part, count in zip(parts, counts) for i in range(count)]
    for w, (part, i) in enumerate(slots):
        projected[w] = jnp.dot(part[i], right, preferred_element_type=jnp.float32).astype(jnp.bfloat16)


def join(ours, theirs, mine, lowest, mixed, outs):
    left = jnp.concatenate([ours.T, theirs.T], axis=1)
    slots = [(out, i) for out in outs for i in range(out.shape[0])]
    blk = left.shape[0]
    for v in range(0, len(slots), 2):
        pair = range(v, min(v + 2, len(slots)))
        right = jnp.concatenate([jnp.concatenate([mine[lowest + u], mixed[u]], axis=0) for u in pair], axis=1)
        both = jnp.dot(left, right, preferred_element_type=jnp.float32)
        for n, u in enumerate(pair):
            out, i = slots[u]
            out[i] = both[:, n * blk:(n + 1) * blk].astype(out.dtype)


def prepare_kernel(here, other, rows, rows_other, states, states_other, local, send, later, live):
    core, inside, _, _ = place()

    def block(site, target, state, choice):
        same = core == site

        def exists(k):
            flag = jnp.where(same, here[:, k:k + 1], other[:, k:k + 1]) > 0
            return flag & inside if k >= 2 else flag

        def of(k):
            both = jnp.where(same, states[target, k], states_other[target, k])
            return jnp.where(exists(k), both, jnp.zeros_like(both))

        return of(state) if state == choice else jnp.where(target == 0, of(state), of(choice))

    send[0] = block(0, core, 3, 3)
    local[0, 0] = block(0, 1 - core, 1, 2)
    local[0, 1] = block(0, 1 - core, 0, 0)
    local[1, 0] = block(1, 1 - core, 1, 2)
    local[1, 1] = block(1, 1 - core, 0, 0)
    send[1] = block(0, core, 2, 1)
    later[0] = block(1, 1 - core, 3, 3)
    later[1] = block(1, 1 - core, 2, 1)
    for site in range(2):
        live[site] = jnp.broadcast_to(jnp.where(core == site, rows[...], rows_other[...]), live.shape[1:])


def behind(sent):
    core, _, from_down, from_up = place()
    return jnp.where(jnp.where(core == 1, from_down, from_up), sent, jnp.zeros_like(sent))


def own_kernel(site, counts, local, mpo, mpo_other, *refs):
    *parts, out_q, out_r, out_spread, projected = refs
    core = lax.axis_index("chain")
    pick = lambda state: jnp.where(core == site, mpo[state], mpo_other[state])
    middle, zero, both, outer = spreads([pick(2 - core), pick(0), pick(3), pick(1 + core)])
    project(parts, counts, jnp.concatenate([local[site, 0], local[site, 1]], axis=1), projected)
    couple(middle, [projected], 0, out_q)
    couple(zero, [projected], out_q.shape[1], out_r)
    out_spread[0] = both
    out_spread[1] = outer


def project_kernel(site, at, sent, part, projected):
    project([part], projected.shape[:1], behind(sent[at]), projected)


def head_kernel(site, at, local, sent, spread, mine, *refs):
    *projected, part, out, mine_projected, mixed = refs
    theirs = behind(sent[at])
    project([part], mine_projected.shape[:1], theirs, mine_projected)
    couple(spread[0], [*projected, mine_projected], 0, mixed)
    join(local[site, 0], theirs, mine, 0, mixed, [out])


def tail_kernel(site, at, lowest, pieces, local, sent, spread, mine, *refs):
    projected, out, mixed = refs[:pieces], refs[-2], refs[-1]
    couple(spread[0], projected, 0, mixed, lowest)
    join(local[site, 0], behind(sent[at]), mine, lowest, mixed, [out])


def keep_kernel(site, at, counts, local, sent, spread, mine, after, *refs):
    parts, refs = refs[:len(counts)], refs[len(counts):]
    *outs, projected, mixed = refs
    theirs = behind(sent[at + 1])
    project(parts, counts, theirs, projected)
    couple(spread[1], [projected], 0, mixed)
    join(local[site, 1], theirs, mine, 0, mixed, outs)


def give_kernel(parts, kept, *refs):
    envs, outs = refs[:parts], refs[parts:]
    core, width = lax.axis_index("chain"), kept.shape[0]
    for v, ((env, i), (out, j)) in enumerate(zip(blocks_of(envs, width), blocks_of(outs, width))):
        out[j] = jnp.where(core == 0, kept[v].astype(jnp.bfloat16), env[i])


def blocks_of(parts, width):
    extra = sum(part.shape[0] for part in parts) - width
    return [(part, i) for n, part in enumerate(parts) for i in range(part.shape[0] - (0 if n else extra))]


def total(site, live, valid, kept, arrived):
    blk = kept.shape[0]
    rows = live[site, 0:1, :]
    inside = (lax.broadcasted_iota(jnp.int32, (blk, blk), 0) < rows) & (lax.broadcasted_iota(jnp.int32, (blk, blk), 1) < rows)
    both = kept.astype(jnp.float32) + jnp.where(valid, arrived.astype(jnp.float32), 0.0)
    return jnp.where(inside, both, 0.0).astype(jnp.bfloat16)


def sum_kernel(lowest, live, arrived, kept, *refs):
    more, out = refs[0], refs[-1]
    core, _, from_down, from_up = place()
    valid = jnp.where(core == 0, from_down, from_up)
    count = arrived.shape[0]
    for v in range(count):
        out[v] = total(0, live, valid, kept[lowest + v], arrived[v])
    for i in range(out.shape[0] - count):
        out[count + i] = more[i]


def pick_kernel(from_down, from_up, out):
    core = lax.axis_index("chain")
    for i in range(out.shape[0]):
        out[i] = jnp.where(core == 0, from_up[i], from_down[i])


def last_kernel(lowest, parts, started, live, from_up_arrived, from_down_arrived, kept, *refs):
    *refs, out, new, sems = refs
    taken, envs = refs[:parts], refs[parts + started:]
    core, _, from_down, from_up = place()
    count, width = from_up_arrived.shape[0], kept.shape[0]
    received = [part[i] for part, i in blocks_of(taken, width)[lowest:lowest + count]]
    slots = blocks_of(envs, width)[lowest:lowest + count]
    steps = [(low, min(low + STEP, count)) for low in range(0, count, STEP)]
    copies = []
    for low, high in steps:
        for v in range(low, high):
            env, i = slots[v]
            zero = total(1, live, from_up, kept[lowest + v], from_up_arrived[v])
            one = total(1, live, from_down, received[v], from_down_arrived[v])
            new[0, v] = jnp.where(core == 0, received[v], zero)
            new[1, v] = jnp.where(core == 0, env[i], one)
        part = pl.ds(low, high - low)
        copies.append(pltpu.make_async_copy(new.at[:, part], out.at[:, pl.ds(lowest + low, high - low)], sems.at[len(copies)]))
        copies[-1].start()
    for copy in copies:
        copy.wait()


VMEM = pl.BlockSpec(memory_space=pltpu.VMEM)
SMEM = pl.BlockSpec(memory_space=pltpu.SMEM)


def call(kernel, out_shape, in_specs, scratch=()):
    single = not isinstance(out_shape, (tuple, list))
    return pl.pallas_call(
        kernel,
        out_shape=out_shape,
        in_specs=in_specs,
        out_specs=VMEM if single else [VMEM] * len(out_shape),
        scratch_shapes=scratch,
        compiler_params=pltpu.CompilerParams(vmem_limit_bytes=24 << 20),
        cost_estimate=pl.CostEstimate(flops=1, bytes_accessed=1, transcendentals=0),
    )


def on_device(env_first, states, mpo, block_rows, present):
    pairs = rings(lax.axis_size("sector"))
    move = lambda value, name: lax.ppermute(value, AXES, pairs[name])
    core = lax.axis_index("chain")
    _, _, width, blk, _ = env_first.shape
    array = lambda *shape, dtype=jnp.bfloat16: jax.ShapeDtypeStruct(shape, dtype)
    blocks = lambda n, dtype=jnp.bfloat16: array(n, blk, blk, dtype=dtype)
    scratch = lambda n, m=1: pltpu.VMEM((n, blk, m * blk), jnp.bfloat16)
    half = blocks(width)
    spread_shape = array(2, width * LO, width * LO)
    lengths = cut(width, BC)
    ends = cut(width, DD)
    starts = lambda counts: [sum(counts[:i]) for i in range(len(counts))]

    env_first = env_first[:, 0]
    states, mpo, rows, here = states[0, :, :, 0], mpo[0], block_rows, present[:, :, 0]
    env = lax.dynamic_index_in_dim(env_first, core, 0, keepdims=False)
    arriving = move(env, "envs")
    states_other, mpo_other, rows_other, other = lax.optimization_barrier(tuple(move(x, "swap") for x in (states, mpo, rows, here)))
    local, send, later, live = call(
        prepare_kernel, [array(2, 2, blk, blk), array(2, blk, blk), array(2, blk, blk), array(2, 8, blk, dtype=jnp.int32)], [VMEM] * 6,
    )(here, other, rows, rows_other, states, states_other)
    sent = move(send, "envs")
    env = lax.optimization_barrier((env, local))[0]
    given = cut(width, EE)
    env = [move(env[low:low + n], "swap") for low, n in zip(starts(given), given)]

    own = lambda site, counts: call(
        functools.partial(own_kernel, site, counts), [half, half, spread_shape], [VMEM] * (3 + len(counts)), [scratch(width, 2)])

    def outgoing(site, at, sent, spread, mine, projected, part, count, counts):
        fixed = (local, sent, spread, mine)
        first, last = call(
            functools.partial(head_kernel, site, at), [blocks(counts[0]), blocks(count)], [VMEM] * (5 + len(projected)), [scratch(counts[0])],
        )(*fixed, *projected, part)
        projected = [*projected, last]
        out = [first]
        for low, n in list(zip(starts(counts), counts))[1:]:
            out.append(call(
                functools.partial(tail_kernel, site, at, low, len(projected)), blocks(n), [VMEM] * (4 + len(projected) + len(out)), [scratch(n)],
            )(*fixed, *projected, *out))
        return out

    mine_q, mine_r, spread = own(0, given)(local, mpo, mpo_other, *env)
    q = outgoing(0, 0, sent, spread, mine_q, [], arriving, width, lengths)
    arrived = [move(part, "partials") for part in q]
    whole = blocks(width, jnp.float32)
    kept = call(functools.partial(keep_kernel, 0, 0, (width,)), whole, [VMEM] * 6, [scratch(width)] * 2)(
        local, sent, spread, mine_r, q[-1], arriving)
    envs = []
    for low, n, part in zip(starts(lengths), lengths, arrived):
        extra = 0 if envs else later.shape[0]
        envs.append(call(functools.partial(sum_kernel, low), blocks(n + extra), [VMEM] * (4 + len(envs)))(live, part, kept, later, *envs))
    arriving = [
        call(pick_kernel, blocks(env.shape[0]), [VMEM] * 2)(move(env, "across"), move(env, "lift")) for env in envs
    ]
    sent, at = arriving[0], lengths[0]

    mine_q, mine_r, spread = own(1, lengths)(local, mpo, mpo_other, *envs)
    early = [
        call(functools.partial(project_kernel, 1, at), blocks(n), [VMEM] * 2)(sent, part) for part, n in zip(arriving[:-1], lengths)
    ]
    q = outgoing(1, at, sent, spread, mine_q, early, arriving[-1], lengths[-1], ends)
    downs = [move(part, "down") for part in q]
    ups = [move(part, "up") for part in q]
    kept = call(functools.partial(keep_kernel, 1, at, lengths), whole, [VMEM] * (5 + len(arriving)), [scratch(width)] * 2)(
        local, sent, spread, mine_r, q[-1], *arriving)
    given = call(functools.partial(give_kernel, len(envs)), [blocks(n) for n in cut(width, GG)], [VMEM] * (1 + len(envs)))(kept, *envs)
    taken = [move(part, "swap") for part in lax.optimization_barrier((given, downs[0]))[0]]
    hbm = pl.BlockSpec(memory_space=pl.ANY)
    result = []
    for i, low in enumerate(starts(ends)):
        result = [pl.pallas_call(
            functools.partial(last_kernel, low, len(taken), len(result)),
            out_shape=array(2, width, blk, blk),
            in_specs=[VMEM] * (4 + len(taken)) + [hbm] * len(result) + [VMEM] * len(envs),
            out_specs=hbm,
            scratch_shapes=[pltpu.VMEM((2, ends[i], blk, blk), jnp.bfloat16), pltpu.SemaphoreType.DMA((-(-ends[i] // STEP),))],
            input_output_aliases={4 + len(taken): 0} if result else {},
            compiler_params=pltpu.CompilerParams(vmem_limit_bytes=24 << 20),
            cost_estimate=pl.CostEstimate(flops=1, bytes_accessed=1, transcendentals=0),
        )(live, ups[i], downs[i], kept, *taken, *result, *envs)]
    return result[0][None, :, None]


def solution(mesh):
    placed = (
        P(None, "sector", None, None, None),
        P("chain", None, None, "sector", None, None),
        P("chain", None, None, None),
        P("chain", "sector"),
        P("chain", None, "sector"),
    )
    return jax.shard_map(
        on_device,
        mesh=mesh,
        in_specs=placed,
        out_specs=P("chain", None, "sector", None, None, None),
        check_vma=False,
    )
```

```python
import functools

import jax
import jax.numpy as jnp
from jax import lax
from jax.experimental import pallas as pl
from jax.experimental.pallas import tpu as pltpu
from jax.sharding import PartitionSpec as P

QD = 4
LO = 16
AXES = ("chain", "sector")
BC = (7, 8)
EE = (8, 7)
DD = (7, 8)
STEP = 3
GG = (6, 6, 3)
ACROSS = [(4, 5), (5, 6), (6, 7), (7, 1), (1, 3), (3, 2), (2, 0), (0, 4)]


def cut(width, shares):
    ends = [round(width * sum(shares[:i]) / sum(shares)) for i in range(len(shares) + 1)]
    return tuple(b - a for a, b in zip(ends, ends[1:]))


def rings(sectors):
    down = lambda k: (k // QD) * QD + (k + 1) % QD
    up = lambda k: (k + QD) % sectors
    stay = lambda k: k

    def pairs(zero, one, cross):
        to_zero, to_one = (sectors, 0) if cross else (0, sectors)
        return [(k, to_zero + zero(k)) for k in range(sectors)] + [(sectors + k, to_one + one(k)) for k in range(sectors)]

    last = sectors - QD
    column = [(sectors + k, sectors + k + QD if k < last else k) for k in range(sectors)]
    column += [(k, k - QD if k >= QD else sectors + k) for k in range(sectors)]
    lift = [(k, k + QD if k < last else sectors + k) for k in range(sectors)]
    lift += [(sectors + k, sectors + k - QD if k >= QD else k) for k in range(sectors)]
    across = [(a // QD * sectors + g + a % QD, b // QD * sectors + g + b % QD) for g in range(0, sectors, QD) for a, b in ACROSS]

    return {
        "lift": lift,
        "across": across,
        "envs": pairs(down, up, True),
        "partials": pairs(down, up, False),
        "up": column,
        "down": pairs(down, stay, True),
        "swap": pairs(stay, stay, True),
    }


def place():
    core, sector = lax.axis_index("chain"), lax.axis_index("sector")
    return core, lax.rem(sector, QD) < QD - 1, lax.rem(sector, QD) > 0, sector >= QD


def spreads(couplings):
    w = couplings[0].shape[0]
    rows = lax.broadcasted_iota(jnp.int32, (w * LO, w), 0) // LO
    pick = (rows == lax.broadcasted_iota(jnp.int32, (w * LO, w), 1)).astype(jnp.bfloat16)
    i = lax.broadcasted_iota(jnp.int32, (w * LO, w * LO), 0) % LO
    j = lax.broadcasted_iota(jnp.int32, (w * LO, w * LO), 1) % LO
    same = i == j

    def spread(mpo):
        tall = lax.dot_general(pick, mpo, (((1,), (1,)), ((), ())), preferred_element_type=jnp.float32).astype(jnp.bfloat16)
        full = lax.dot_general(tall, pick, (((1,), (1,)), ((), ())), preferred_element_type=jnp.float32)
        return jnp.where(same, full, 0.0).astype(jnp.bfloat16)

    return [spread(mpo) for mpo in couplings]


def couple(coupling, projected, column, out, lowest=0):
    count, blk = out.shape[0], out.shape[1]
    coupling = coupling[lowest * LO:(lowest + count) * LO]

    def part(a):
        pieces = [p[:, a:a + LO, column:column + blk].reshape(p.shape[0] * LO, blk) for p in projected]
        return pieces[0] if len(pieces) == 1 else jnp.concatenate(pieces, axis=0)

    for a in range(0, blk, 2 * LO):
        both = jnp.concatenate([part(a), part(a + LO)], axis=1)
        mixed = jnp.dot(coupling, both, preferred_element_type=jnp.float32).astype(out.dtype)
        out[:, a:a + LO, :] = mixed[:, :blk].reshape(count, LO, blk)
        out[:, a + LO:a + 2 * LO, :] = mixed[:, blk:].reshape(count, LO, blk)


def project(parts, counts, right, projected):
    slots = [(part, i) for part, count in zip(parts, counts) for i in range(count)]
    for w, (part, i) in enumerate(slots):
        projected[w] = jnp.dot(part[i], right, preferred_element_type=jnp.float32).astype(jnp.bfloat16)


def join(ours, theirs, mine, lowest, mixed, outs):
    left = jnp.concatenate([ours.T, theirs.T], axis=1)
    slots = [(out, i) for out in outs for i in range(out.shape[0])]
    blk = left.shape[0]
    for v in range(0, len(slots), 2):
        pair = range(v, min(v + 2, len(slots)))
        right = jnp.concatenate([jnp.concatenate([mine[lowest + u], mixed[u]], axis=0) for u in pair], axis=1)
        both = jnp.dot(left, right, preferred_element_type=jnp.float32)
        for n, u in enumerate(pair):
            out, i = slots[u]
            out[i] = both[:, n * blk:(n + 1) * blk].astype(out.dtype)


def prepare_kernel(here, other, rows, rows_other, states, states_other, local, send, later, live):
    core, inside, _, _ = place()

    def block(site, target, state, choice):
        same = core == site

        def exists(k):
            flag = jnp.where(same, here[:, k:k + 1], other[:, k:k + 1]) > 0
            return flag & inside if k >= 2 else flag

        def of(k):
            both = jnp.where(same, states[target, k], states_other[target, k])
            return jnp.where(exists(k), both, jnp.zeros_like(both))

        return of(state) if state == choice else jnp.where(target == 0, of(state), of(choice))

    send[0] = block(0, core, 3, 3)
    local[0, 0] = block(0, 1 - core, 1, 2)
    local[0, 1] = block(0, 1 - core, 0, 0)
    local[1, 0] = block(1, 1 - core, 1, 2)
    local[1, 1] = block(1, 1 - core, 0, 0)
    send[1] = block(0, core, 2, 1)
    later[0] = block(1, 1 - core, 3, 3)
    later[1] = block(1, 1 - core, 2, 1)
    for site in range(2):
        live[site] = jnp.broadcast_to(jnp.where(core == site, rows[...], rows_other[...]), live.shape[1:])


def behind(sent):
    core, _, from_down, from_up = place()
    return jnp.where(jnp.where(core == 1, from_down, from_up), sent, jnp.zeros_like(sent))


def own_kernel(site, counts, local, mpo, mpo_other, *refs):
    *parts, out_q, out_r, out_spread, projected = refs
    core = lax.axis_index("chain")
    pick = lambda state: jnp.where(core == site, mpo[state], mpo_other[state])
    middle, zero, both, outer = spreads([pick(2 - core), pick(0), pick(3), pick(1 + core)])
    project(parts, counts, jnp.concatenate([local[site, 0], local[site, 1]], axis=1), projected)
    couple(middle, [projected], 0, out_q)
    couple(zero, [projected], out_q.shape[1], out_r)
    out_spread[0] = both
    out_spread[1] = outer


def project_kernel(site, at, sent, part, projected):
    project([part], projected.shape[:1], behind(sent[at]), projected)


def head_kernel(site, at, local, sent, spread, mine, *refs):
    *projected, part, out, mine_projected, mixed = refs
    theirs = behind(sent[at])
    project([part], mine_projected.shape[:1], theirs, mine_projected)
    couple(spread[0], [*projected, mine_projected], 0, mixed)
    join(local[site, 0], theirs, mine, 0, mixed, [out])


def tail_kernel(site, at, lowest, pieces, local, sent, spread, mine, *refs):
    projected, out, mixed = refs[:pieces], refs[-2], refs[-1]
    couple(spread[0], projected, 0, mixed, lowest)
    join(local[site, 0], behind(sent[at]), mine, lowest, mixed, [out])


def keep_kernel(site, at, counts, local, sent, spread, mine, after, *refs):
    parts, refs = refs[:len(counts)], refs[len(counts):]
    *outs, projected, mixed = refs
    theirs = behind(sent[at + 1])
    project(parts, counts, theirs, projected)
    couple(spread[1], [projected], 0, mixed)
    join(local[site, 1], theirs, mine, 0, mixed, outs)


def give_kernel(parts, kept, *refs):
    envs, outs = refs[:parts], refs[parts:]
    core, width = lax.axis_index("chain"), kept.shape[0]
    for v, ((env, i), (out, j)) in enumerate(zip(blocks_of(envs, width), blocks_of(outs, width))):
        out[j] = jnp.where(core == 0, kept[v].astype(jnp.bfloat16), env[i])


def blocks_of(parts, width):
    extra = sum(part.shape[0] for part in parts) - width
    return [(part, i) for n, part in enumerate(parts) for i in range(part.shape[0] - (0 if n else extra))]


def total(site, live, valid, kept, arrived):
    blk = kept.shape[0]
    rows = live[site, 0:1, :]
    inside = (lax.broadcasted_iota(jnp.int32, (blk, blk), 0) < rows) & (lax.broadcasted_iota(jnp.int32, (blk, blk), 1) < rows)
    both = kept.astype(jnp.float32) + jnp.where(valid, arrived.astype(jnp.float32), 0.0)
    return jnp.where(inside, both, 0.0).astype(jnp.bfloat16)


def sum_kernel(lowest, live, arrived, kept, *refs):
    more, out = refs[0], refs[-1]
    core, _, from_down, from_up = place()
    valid = jnp.where(core == 0, from_down, from_up)
    count = arrived.shape[0]
    for v in range(count):
        out[v] = total(0, live, valid, kept[lowest + v], arrived[v])
    for i in range(out.shape[0] - count):
        out[count + i] = more[i]


def pick_kernel(from_down, from_up, out):
    core = lax.axis_index("chain")
    for i in range(out.shape[0]):
        out[i] = jnp.where(core == 0, from_up[i], from_down[i])


def last_kernel(lowest, parts, started, live, from_up_arrived, from_down_arrived, kept, *refs):
    *refs, out, new, sems = refs
    taken, envs = refs[:parts], refs[parts + started:]
    core, _, from_down, from_up = place()
    count, width = from_up_arrived.shape[0], kept.shape[0]
    received = [part[i] for part, i in blocks_of(taken, width)[lowest:lowest + count]]
    slots = blocks_of(envs, width)[lowest:lowest + count]
    steps = [(low, min(low + STEP, count)) for low in range(0, count, STEP)]
    copies = []
    for low, high in steps:
        for v in range(low, high):
            env, i = slots[v]
            zero = total(1, live, from_up, kept[lowest + v], from_up_arrived[v])
            one = total(1, live, from_down, received[v], from_down_arrived[v])
            new[0, v] = jnp.where(core == 0, received[v], zero)
            new[1, v] = jnp.where(core == 0, env[i], one)
        part = pl.ds(low, high - low)
        copies.append(pltpu.make_async_copy(new.at[:, part], out.at[:, pl.ds(lowest + low, high - low)], sems.at[len(copies)]))
        copies[-1].start()
    for copy in copies:
        copy.wait()


VMEM = pl.BlockSpec(memory_space=pltpu.VMEM)
SMEM = pl.BlockSpec(memory_space=pltpu.SMEM)


def call(kernel, out_shape, in_specs, scratch=()):
    single = not isinstance(out_shape, (tuple, list))
    return pl.pallas_call(
        kernel,
        out_shape=out_shape,
        in_specs=in_specs,
        out_specs=VMEM if single else [VMEM] * len(out_shape),
        scratch_shapes=scratch,
        compiler_params=pltpu.CompilerParams(vmem_limit_bytes=24 << 20),
        cost_estimate=pl.CostEstimate(flops=1, bytes_accessed=1, transcendentals=0),
    )


def on_device(env_first, states, mpo, block_rows, present):
    pairs = rings(lax.axis_size("sector"))
    move = lambda value, name: lax.ppermute(value, AXES, pairs[name])
    core = lax.axis_index("chain")
    _, _, width, blk, _ = env_first.shape
    array = lambda *shape, dtype=jnp.bfloat16: jax.ShapeDtypeStruct(shape, dtype)
    blocks = lambda n, dtype=jnp.bfloat16: array(n, blk, blk, dtype=dtype)
    scratch = lambda n, m=1: pltpu.VMEM((n, blk, m * blk), jnp.bfloat16)
    half = blocks(width)
    spread_shape = array(2, width * LO, width * LO)
    lengths = cut(width, BC)
    ends = cut(width, DD)
    starts = lambda counts: [sum(counts[:i]) for i in range(len(counts))]

    env_first = env_first[:, 0]
    states, mpo, rows, here = states[0, :, :, 0], mpo[0], block_rows, present[:, :, 0]
    env = lax.dynamic_index_in_dim(env_first, core, 0, keepdims=False)
    arriving = move(env, "envs")
    states_other, mpo_other, rows_other, other = lax.optimization_barrier(tuple(move(x, "swap") for x in (states, mpo, rows, here)))
    local, send, later, live = call(
        prepare_kernel, [array(2, 2, blk, blk), array(2, blk, blk), array(2, blk, blk), array(2, 8, blk, dtype=jnp.int32)], [VMEM] * 6,
    )(here, other, rows, rows_other, states, states_other)
    sent = move(send, "envs")
    env = lax.optimization_barrier((env, local))[0]
    given = cut(width, EE)
    env = [move(env[low:low + n], "swap") for low, n in zip(starts(given), given)]

    own = lambda site, counts: call(
        functools.partial(own_kernel, site, counts), [half, half, spread_shape], [VMEM] * (3 + len(counts)), [scratch(width, 2)])

    def outgoing(site, at, sent, spread, mine, projected, part, count, counts):
        fixed = (local, sent, spread, mine)
        first, last = call(
            functools.partial(head_kernel, site, at), [blocks(counts[0]), blocks(count)], [VMEM] * (5 + len(projected)), [scratch(counts[0])],
        )(*fixed, *projected, part)
        projected = [*projected, last]
        out = [first]
        for low, n in list(zip(starts(counts), counts))[1:]:
            out.append(call(
                functools.partial(tail_kernel, site, at, low, len(projected)), blocks(n), [VMEM] * (4 + len(projected) + len(out)), [scratch(n)],
            )(*fixed, *projected, *out))
        return out

    mine_q, mine_r, spread = own(0, given)(local, mpo, mpo_other, *env)
    q = outgoing(0, 0, sent, spread, mine_q, [], arriving, width, lengths)
    arrived = [move(part, "partials") for part in q]
    whole = blocks(width, jnp.float32)
    kept = call(functools.partial(keep_kernel, 0, 0, (width,)), whole, [VMEM] * 6, [scratch(width)] * 2)(
        local, sent, spread, mine_r, q[-1], arriving)
    envs = []
    for low, n, part in zip(starts(lengths), lengths, arrived):
        extra = 0 if envs else later.shape[0]
        envs.append(call(functools.partial(sum_kernel, low), blocks(n + extra), [VMEM] * (4 + len(envs)))(live, part, kept, later, *envs))
    arriving = [
        call(pick_kernel, blocks(env.shape[0]), [VMEM] * 2)(move(env, "across"), move(env, "lift")) for env in envs
    ]
    sent, at = arriving[0], lengths[0]

    mine_q, mine_r, spread = own(1, lengths)(local, mpo, mpo_other, *envs)
    early = [
        call(functools.partial(project_kernel, 1, at), blocks(n), [VMEM] * 2)(sent, part) for part, n in zip(arriving[:-1], lengths)
    ]
    q = outgoing(1, at, sent, spread, mine_q, early, arriving[-1], lengths[-1], ends)
    downs = [move(part, "down") for part in q]
    ups = [move(part, "up") for part in q]
    kept = call(functools.partial(keep_kernel, 1, at, lengths), whole, [VMEM] * (5 + len(arriving)), [scratch(width)] * 2)(
        local, sent, spread, mine_r, q[-1], *arriving)
    given = call(functools.partial(give_kernel, len(envs)), [blocks(n) for n in cut(width, GG)], [VMEM] * (1 + len(envs)))(kept, *envs)
    taken = [move(part, "swap") for part in lax.optimization_barrier((given, downs[0]))[0]]
    hbm = pl.BlockSpec(memory_space=pl.ANY)
    result = []
    for i, low in enumerate(starts(ends)):
        result = [pl.pallas_call(
            functools.partial(last_kernel, low, len(taken), len(result)),
            out_shape=array(2, width, blk, blk),
            in_specs=[VMEM] * (4 + len(taken)) + [hbm] * len(result) + [VMEM] * len(envs),
            out_specs=hbm,
            scratch_shapes=[pltpu.VMEM((2, ends[i], blk, blk), jnp.bfloat16), pltpu.SemaphoreType.DMA((-(-ends[i] // STEP),))],
            input_output_aliases={4 + len(taken): 0} if result else {},
            compiler_params=pltpu.CompilerParams(vmem_limit_bytes=24 << 20),
            cost_estimate=pl.CostEstimate(flops=1, bytes_accessed=1, transcendentals=0),
        )(live, ups[i], downs[i], kept, *taken, *result, *envs)]
    return result[0][None, :, None]


def solution(mesh):
    placed = (
        P(None, "sector", None, None, None),
        P("chain", None, None, "sector", None, None),
        P("chain", None, None, None),
        P("chain", "sector"),
        P("chain", None, "sector"),
    )
    return jax.shard_map(
        on_device,
        mesh=mesh,
        in_specs=placed,
        out_specs=P("chain", None, "sector", None, None, None),
        check_vma=False,
    )
```
